256 devices in a mesh: pipe: 8 (over y_hi, x), fsdp: 16 (over z, core), rep: 2 (over y_lo).
Axes of the slice: x: 4, y: 4 (y_hi: 2, y_lo: 2; y = y_hi * 2 + y_lo), z: 8, core: 2. Of those that a mesh axis runs over, the one named last changes fastest.
Arguments:
- activations: bfloat16 [8, 2, 2048, 8192], P('pipe', 'rep', 'fsdp'), may hold values from -6 to 6
- query_rows: bfloat16 [8, 2, 2048, 8192], P('pipe', 'rep', 'fsdp'), may hold values from -6 to 6
- key_rows: bfloat16 [8, 2, 2048, 512], P('pipe', 'rep', 'fsdp'), may hold values from -6 to 6
- out_grad: bfloat16 [8, 2, 2048, 8192], P('pipe', 'rep', 'fsdp'), may hold values from -6 to 6
- value_weight: bfloat16 [8, 8192, 512], P('pipe', 'fsdp'), may hold values from -0.0625 to 0.0625
- doc_lengths: int32 [2, 4], P('rep'), may hold values from 1 to 1024, 2048 in all within a row
Outputs:
- upstream_grad: bfloat16 [8, 2, 2048, 8192], P('pipe', 'rep', 'fsdp')
- query_grad: bfloat16 [8, 2, 2048, 8192], P('pipe', 'rep', 'fsdp')
- key_grad: bfloat16 [8, 2, 2048, 512], P('pipe', 'rep', 'fsdp')
- weight_grad: bfloat16 [8, 8192, 512], P('pipe', 'fsdp')
The draws below stay inside these ranges and needn't reach their ends.
Inputs may be any that keep to these rules, and one draw needn't show every extreme that they name: `doc_lengths`: each row sums to 2048; each row's longest document has exactly 1024 tokens.
All inputs are finite; a program needn't handle non-finite values.
Results may differ from the reference program's by a relative error of at most 0.027.
Values may be sent and summed in bfloat16 or wider, within the bound.
No kernel may reach another device: no remote copies, remote signals or barrier semaphores. Data moves between devices by JAX's collectives and lax.ppermute only.
A program may use at most 128 MiB of HBM per device.

```python
import math
import jax
import jax.numpy as jnp
import numpy as np
from jax import lax

D = 8192
HQ = 64
KV = 4
HD = 128
DOCS = 4
TOK_DEV = 128
SECTIONS = 8
MB = 2
PACK = 2048
QD = 8192
KVD = 512


def with_spikes(array, own_key, source, target, blocks, factor):
    owner, partner = [(jnp.arange(array.shape[axis_at]) // (array.shape[axis_at] // blocks)).reshape([-1 if axis == axis_at else 1 for axis in range(array.ndim)]) for axis_at in (source, target)]
    chosen = jax.random.permutation(own_key, blocks)[partner]
    strong = (owner == chosen) | (owner == (partner + blocks // 2) % blocks)
    return jnp.where(strong, factor * array, array)


def levels(stream_key, extent, shards, low, largest):
    def one(axis_at, blocks):
        heights = jax.random.uniform(jax.random.fold_in(jax.random.fold_in(stream_key, 6), axis_at), (blocks,), jnp.float32, low / len(shards), largest / len(shards))
        return jnp.repeat(jnp.exp(heights), extent[axis_at] // blocks).reshape((-1,) + (1,) * (len(extent) - axis_at - 1))

    loudness = one(*shards[0])
    for cut in shards[1:]:
        loudness = loudness * one(*cut)
    return loudness


def split_up(amount, total, reach, slope):
    portions = [(1 << 20) // math.isqrt(grade ** slope) + 1 for grade in range(2, amount + 1)]
    rest, counts = total - reach - (amount - 1), [1] * (amount - 1)
    while rest > 0:
        candidates = [i for i in range(amount - 1) if counts[i] < reach]
        mass, remaining = sum([portions[i] for i in candidates]), rest
        for i in candidates:
            addition = min(reach - counts[i], max(1, remaining * portions[i] // mass), rest)
            counts[i] = counts[i] + addition
            rest = rest - addition
    return np.array([reach] + counts)


def uneven(stream_key, amount, total, most, skew):
    if amount == 2:
        one = jax.random.randint(stream_key, (), max(1, total - most), min(most, total - 1) + 1)
        return jnp.stack([one, total - one])
    sizes = jnp.asarray(split_up(amount, total, most, skew), jnp.int32)
    twos = (amount - 1) // 2
    source_of, taker = sizes[1:1 + 2 * twos:2], sizes[2:2 + 2 * twos:2]
    room = jnp.minimum(source_of - 1, most - taker)
    moved = jax.random.randint(jax.random.fold_in(stream_key, 1), (twos,), 0, 1 << 20) % (room + 1)
    sizes = sizes.at[1:1 + 2 * twos:2].set(source_of - moved).at[2:2 + 2 * twos:2].set(taker + moved)
    return sizes[jax.random.permutation(jax.random.fold_in(stream_key, 2), amount)]


def bell_draw(stream_key, extent, width, bound, split=(), kind=jnp.bfloat16):
    factor_of = levels(stream_key, extent, split, -0.22, 0.18) if split else 1.0
    array = jax.random.normal(stream_key, extent, jnp.float32) * width * factor_of
    return jnp.minimum(jnp.maximum(array, -bound), bound).astype(kind)


def noise_with(stream_key, extent, spread, bound, split, heavy, kind=jnp.bfloat16):
    array = spread * jax.random.normal(stream_key, extent, jnp.float32)
    if split:
        array = array * levels(stream_key, extent, split, -0.22, 0.18)
    return jnp.clip(with_spikes(array, jax.random.fold_in(stream_key, 3), *heavy), -bound, bound).astype(kind)


def setup_inputs(seed: int = 0) -> dict:
    key_list = jax.random.split(jax.random.key(seed), 7)
    return {
        "activations": noise_with(key_list[0], (SECTIONS, MB, PACK, D), 1.0, 6.0, ((0, 8), (1, 2), (2, 16)), (2, 3, 16, 2.0)),
        "query_rows": bell_draw(key_list[1], (SECTIONS, MB, PACK, QD), 1.0, 6.0, ((0, 8), (1, 2), (2, 16))),
        "key_rows": bell_draw(key_list[2], (SECTIONS, MB, PACK, KVD), 1.0, 6.0, ((0, 8), (1, 2), (2, 16))),
        "out_grad": bell_draw(key_list[3], (SECTIONS, MB, PACK, QD), 1.0, 6.0, ((0, 8), (1, 2), (2, 16))),
        "value_weight": bell_draw(key_list[4], (SECTIONS, D, KVD), D ** -0.5, 0.0625, ((0, 8), (1, 16))),
        "doc_lengths": jax.vmap(lambda own: uneven(own, DOCS, PACK, PACK // 2, 2))(jax.random.split(key_list[5], MB)).reshape((MB, DOCS)).astype(jnp.int32),
    }


def to_bf16(values_in):
    return lax.optimization_barrier(values_in.astype(jnp.bfloat16)).astype(jnp.float32)


def attention_grads(query_block, grad_block, key_all, value_all, query_start, lengths):
    count_rows = query_block.shape[0]
    key_count = key_all.shape[0]
    block_width = min(512, key_count)
    block_total = key_count // block_width
    group_size = HQ // KV
    score_scale = HD ** -0.5
    query_heads = query_block.astype(jnp.float32).reshape(count_rows, KV, group_size, HD)
    grad_heads = grad_block.astype(jnp.float32).reshape(count_rows, KV, group_size, HD)
    doc_ends = jnp.cumsum(lengths).astype(jnp.int32)
    doc_starts = doc_ends - lengths
    query_pos = query_start + jnp.arange(count_rows, dtype=jnp.int32)
    query_seg = jnp.sum((query_pos[:, None] >= doc_ends[None, :]).astype(jnp.int32), axis=1)
    first_start = jnp.max(jnp.where(doc_starts <= query_start, doc_starts, 0))
    last_row = query_start + count_rows - 1

    def block_scores(block):
        begin = block * block_width
        key_block = lax.dynamic_slice_in_dim(key_all, begin, block_width, 0).astype(jnp.float32).reshape(block_width, KV, HD)
        value_block = lax.dynamic_slice_in_dim(value_all, begin, block_width, 0).astype(jnp.float32).reshape(block_width, KV, HD)
        key_pos = begin + jnp.arange(block_width, dtype=jnp.int32)
        key_seg = jnp.sum((key_pos[:, None] >= doc_ends[None, :]).astype(jnp.int32), axis=1)
        visible = (query_seg[:, None] == key_seg[None, :]) & (key_pos[None, :] <= query_pos[:, None])
        scores = jnp.einsum('tkgd,skd->tkgs', query_heads, key_block) * score_scale
        numer = jnp.where(visible[:, None, None, :], jnp.exp(scores), 0.0)
        return key_block, value_block, numer

    def is_active(block):
        begin = block * block_width
        return (begin <= last_row) & (begin + block_width - 1 >= first_start)

    def first_pass(block, carry):
        def compute(state):
            totals, weighted = state
            key_block, value_block, numer = block_scores(block)
            return (totals + jnp.sum(numer, axis=-1), weighted + jnp.einsum('tkgs,skd->tkgd', to_bf16(numer), value_block))
        return lax.cond(is_active(block), compute, lambda state: state, carry)

    zero_tot = jnp.zeros((count_rows, KV, group_size), jnp.float32)
    zero_sum = jnp.zeros((count_rows, KV, group_size, HD), jnp.float32)
    totals, weighted = lax.fori_loop(0, block_total, first_pass, (zero_tot, zero_sum))
    delta = jnp.sum(grad_heads * (weighted / totals[..., None]), axis=-1)

    def second_pass(block, carry):
        def compute(state):
            query_acc, key_acc, value_acc = state
            key_block, value_block, numer = block_scores(block)
            probs = numer / totals[..., None]
            value_part = jnp.einsum('tkgs,tkgd->skd', to_bf16(probs), grad_heads)
            dprobs = jnp.einsum('tkgd,skd->tkgs', grad_heads, value_block)
            dscores = to_bf16(probs * (dprobs - delta[..., None]) * score_scale)
            query_acc = query_acc + jnp.einsum('tkgs,skd->tkgd', dscores, key_block)
            key_part = jnp.einsum('tkgs,tkgd->skd', dscores, query_heads)
            begin = block * block_width
            key_acc = lax.dynamic_update_slice_in_dim(key_acc, key_part.reshape(block_width, KV * HD), begin, 0)
            value_acc = lax.dynamic_update_slice_in_dim(value_acc, value_part.reshape(block_width, KV * HD), begin, 0)
            return query_acc, key_acc, value_acc
        return lax.cond(is_active(block), compute, lambda state: state, carry)

    zero_keys = jnp.zeros((key_count, KV * HD), jnp.float32)
    query_acc, key_acc, value_acc = lax.fori_loop(0, block_total, second_pass, (zero_sum, zero_keys, zero_keys))
    return query_acc.reshape(count_rows, HQ * HD), key_acc, value_acc


def reference(activations, query_rows, key_rows, out_grad, value_weight, doc_lengths):
    def one_section(section_args):
        section_act, section_query, section_key, section_grad, section_weight = section_args

        def one_pack(pack_args):
            inputs, queries, keys, grads, lengths = pack_args
            values = jnp.dot(inputs, section_weight, preferred_element_type=jnp.float32).astype(jnp.bfloat16)

            def query_step(carry, index_block):
                key_sum, value_sum = carry
                begin = (index_block * TOK_DEV).astype(jnp.int32)
                query_block = lax.dynamic_slice_in_dim(queries, begin, TOK_DEV, 0)
                grad_block = lax.dynamic_slice_in_dim(grads, begin, TOK_DEV, 0)
                query_out, key_part, value_part = attention_grads(query_block, grad_block, keys, values, begin, lengths)
                return (key_sum + to_bf16(key_part), value_sum + to_bf16(value_part)), query_out.astype(jnp.bfloat16)

            zero_keys = jnp.zeros((PACK, KV * HD), jnp.float32)
            (key_sum, value_sum), query_out = lax.scan(query_step, (zero_keys, zero_keys), jnp.arange(PACK // TOK_DEV, dtype=jnp.int32))
            key_grad = key_sum.astype(jnp.bfloat16)
            value_grad = value_sum.astype(jnp.bfloat16)
            input_grad = lax.dot_general(value_grad, section_weight, (((1,), (1,)), ((), ())), preferred_element_type=jnp.float32).astype(jnp.bfloat16)

            def weight_step(total_acc, index_block):
                begin = (index_block * TOK_DEV).astype(jnp.int32)
                input_block = lax.dynamic_slice_in_dim(inputs, begin, TOK_DEV, 0)
                value_block = lax.dynamic_slice_in_dim(value_grad, begin, TOK_DEV, 0)
                term = lax.dot_general(input_block, value_block, (((0,), (0,)), ((), ())), preferred_element_type=jnp.float32)
                return total_acc + to_bf16(term), None

            weight_sum, unused = lax.scan(weight_step, jnp.zeros((D, KV * HD), jnp.float32), jnp.arange(PACK // TOK_DEV, dtype=jnp.int32))
            return input_grad, query_out.reshape(PACK, HQ * HD), key_grad, weight_sum

        input_grad, query_out, key_grad, weight_sums = lax.map(one_pack, (section_act, section_query, section_key, section_grad, doc_lengths))
        return input_grad, query_out, key_grad, jnp.sum(weight_sums, axis=0).astype(jnp.bfloat16)

    input_grad, query_grad, key_grad, weight_grad = lax.map(one_section, (activations, query_rows, key_rows, out_grad, value_weight))
    upstream_grad = jnp.concatenate([input_grad[1:], jnp.zeros_like(input_grad[:1])], axis=0)
    return upstream_grad, query_grad, key_grad, weight_grad
```

```python
import jax
import jax.numpy as jnp
from jax import lax
from jax.experimental import pallas as pl
from jax.experimental.pallas import tpu as pltpu
from jax.sharding import PartitionSpec as P

HQ = 64
KV = 4
HD = 128
DOCS = 4
TOK = 128
LONGEST = 1024
BACK = LONGEST // TOK
BLOCKS = BACK + 1
HOPS = BACK // 2
WINDOW = BLOCKS * TOK
GROUP = HQ // KV
PAIRS = GROUP // 2
STEP_PAIRS = 2
STEPS = PAIRS // STEP_PAIRS
SCALE = HD ** (-0.5)
LOG2E = 1.4426950408889634
MASKED = -1e30
NT = (((1,), (1,)), ((), ()))
NN = (((1,), (0,)), ((), ()))
QUAD = ((0, 0), (1, 0), (0, 1), (1, 1))


def dot(left, right, numbers):
    return lax.dot_general(left, right, numbers, preferred_element_type=jnp.float32)


def stacked(ref, pair):
    first = 2 * pair * HD
    return jnp.concatenate([ref[:, first : first + HD], ref[:, first + HD : first + 2 * HD]], axis=0)


def probs_kernel(info_ref, query_ref, grad_ref, key_ref, probs_ref, value_ref, bias_ref, *score_refs):
    group, step = pl.program_id(0), pl.program_id(1)

    @pl.when((group == 0) & (step == 0))
    def _():
        begin = info_ref[0]
        query_pos = begin + lax.broadcasted_iota(jnp.int32, (1, TOK), 1)
        doc_start = jnp.zeros((1, TOK), jnp.int32)
        doc_end = 0
        for doc in range(DOCS):
            doc_end = doc_end + info_ref[1 + doc]
            doc_start = jnp.where(query_pos >= doc_end, doc_end, doc_start)
        key_pos = begin - BACK * TOK + lax.broadcasted_iota(jnp.int32, (WINDOW, TOK), 0)
        visible = (key_pos >= doc_start) & (key_pos <= query_pos)
        bias_ref[...] = jnp.where(visible, 0.0, MASKED)

    @pl.when(step == 0)
    def _():
        value_ref[...] = jnp.zeros_like(value_ref)

    for pair in range(STEP_PAIRS):
        score_ref = score_refs[pair]
        query_pair = stacked(query_ref, pair)
        grad_pair = stacked(grad_ref, pair)
        most = jnp.full((1, 2 * TOK), MASKED, jnp.float32)
        for block in range(BLOCKS):
            rows = slice(block * TOK, (block + 1) * TOK)
            bias = bias_ref[rows, :]
            scores = dot(key_ref[rows, :], query_pair, NT) * (SCALE * LOG2E) + jnp.concatenate([bias, bias], axis=1)
            score_ref[rows, :] = scores
            most = jnp.maximum(most, jnp.max(scores, axis=0, keepdims=True))
        total = jnp.zeros((1, 2 * TOK), jnp.float32)
        for block in range(BLOCKS):
            rows = slice(block * TOK, (block + 1) * TOK)
            numer = jnp.exp2(score_ref[rows, :] - most)
            score_ref[rows, :] = numer
            total = total + jnp.sum(numer, axis=0, keepdims=True)
        inverse = 1.0 / total
        for block in range(BLOCKS):
            rows = slice(block * TOK, (block + 1) * TOK)
            probs = (score_ref[rows, :] * inverse).astype(jnp.bfloat16)
            probs_ref[pair, rows, :] = probs
            value_ref[rows, :] += dot(probs, grad_pair, NN)


def grads_kernel(query_ref, grad_ref, key_ref, value_ref, probs_ref, query_out_ref, key_out_ref, flip_ref, *scratch):
    step = pl.program_id(1)
    dprobs_refs, dscores_refs = scratch[:STEP_PAIRS], scratch[STEP_PAIRS:]

    @pl.when(step == 0)
    def _():
        key_out_ref[...] = jnp.zeros_like(key_out_ref)
        for block in range(BLOCKS):
            rows = slice(block * TOK, (block + 1) * TOK)
            flip_ref[:, rows] = key_ref[rows, :].T

    for pair in range(STEP_PAIRS):
        dprobs_ref, dscores_ref = dprobs_refs[pair], dscores_refs[pair]
        query_pair = stacked(query_ref, pair)
        grad_pair = stacked(grad_ref, pair)
        delta = jnp.zeros((1, 2 * TOK), jnp.float32)
        for block in range(BLOCKS):
            rows = slice(block * TOK, (block + 1) * TOK)
            dprobs = dot(value_ref[rows, :], grad_pair, NT)
            dprobs_ref[rows, :] = dprobs
            delta = delta + jnp.sum(probs_ref[pair, rows, :].astype(jnp.float32) * dprobs, axis=0, keepdims=True)
        for block in range(BLOCKS):
            rows = slice(block * TOK, (block + 1) * TOK)
            probs = probs_ref[pair, rows, :].astype(jnp.float32)
            dscores = (probs * (dprobs_ref[rows, :] - delta)).astype(jnp.bfloat16)
            dscores_ref[rows, :] = dscores
            key_out_ref[rows, :] += dot(dscores, query_pair, NN)
        flipped = dot(flip_ref[...], dscores_ref[...], NN) * SCALE
        for half in range(2):
            columns = slice((2 * pair + half) * HD, (2 * pair + half + 1) * HD)
            query_out_ref[:, columns] = flipped[:, half * TOK : (half + 1) * TOK].T.astype(jnp.bfloat16)


def head_spec():
    return pl.BlockSpec((TOK, 2 * STEP_PAIRS * HD), lambda group, step: (0, group * STEPS + step))


def window_spec():
    return pl.BlockSpec((WINDOW, HD), lambda group, step: (0, group))


def probs_spec():
    return pl.BlockSpec((STEP_PAIRS, WINDOW, 2 * TOK), lambda group, step: (group * STEPS + step, 0, 0))


def probs_and_value_grad(info, queries, grads, key_window):
    return pl.pallas_call(
        probs_kernel,
        grid=(KV, STEPS),
        in_specs=[pl.BlockSpec(memory_space=pltpu.SMEM), head_spec(), head_spec(), window_spec()],
        out_specs=[probs_spec(), window_spec()],
        out_shape=[
            jax.ShapeDtypeStruct((HQ // 2, WINDOW, 2 * TOK), jnp.bfloat16),
            jax.ShapeDtypeStruct((WINDOW, KV * HD), jnp.float32),
        ],
        scratch_shapes=[pltpu.VMEM((WINDOW, TOK), jnp.float32)]
        + [pltpu.VMEM((WINDOW, 2 * TOK), jnp.float32)] * STEP_PAIRS,
        compiler_params=pltpu.CompilerParams(vmem_limit_bytes=40 * 1024 * 1024),
        cost_estimate=pl.CostEstimate(
            flops=2 * 2 * HQ * TOK * WINDOW * HD, bytes_accessed=26 << 20, transcendentals=HQ * TOK * WINDOW
        ),
    )(info, queries, grads, key_window)


def query_and_key_grad(queries, grads, key_window, value_window, probs):
    return pl.pallas_call(
        grads_kernel,
        grid=(KV, STEPS),
        in_specs=[head_spec(), head_spec(), window_spec(), window_spec(), probs_spec()],
        out_specs=[head_spec(), window_spec()],
        out_shape=[
            jax.ShapeDtypeStruct((TOK, HQ * HD), jnp.bfloat16),
            jax.ShapeDtypeStruct((WINDOW, KV * HD), jnp.float32),
        ],
        scratch_shapes=[pltpu.VMEM((HD, WINDOW), jnp.bfloat16)]
        + [pltpu.VMEM((WINDOW, 2 * TOK), jnp.float32)] * STEP_PAIRS
        + [pltpu.VMEM((WINDOW, 2 * TOK), jnp.bfloat16)] * STEP_PAIRS,
        compiler_params=pltpu.CompilerParams(vmem_limit_bytes=40 * 1024 * 1024),
        cost_estimate=pl.CostEstimate(
            flops=3 * 2 * HQ * TOK * WINDOW * HD, bytes_accessed=30 << 20, transcendentals=0
        ),
    )(queries, grads, key_window, value_window, probs)


def shifted(value, axis, steps):
    count = lax.axis_size(axis)
    initial, last = (max(0, -steps), min(count, count - steps))
    return lax.ppermute(value, axis, [(source, source + steps) for source in range(initial, last)])


def permuted(value, steps):
    count = lax.axis_size("fsdp")
    return lax.ppermute(value, "fsdp", [(source, (source + steps) % count) for source in range(count)])


def core_swapped(value):
    count = lax.axis_size("fsdp")
    return lax.ppermute(value, "fsdp", [(source, source ^ 1) for source in range(count)])


def window_of(block, odd):
    own = [block] + [permuted(block, 2 * hop) for hop in range(1, HOPS + 1)]
    given = jnp.concatenate([lax.select(odd, own[hop + 1], own[hop]) for hop in range(HOPS)], axis=0)
    taken = core_swapped(given)
    pieces = [own[HOPS]]
    for hop in reversed(range(HOPS)):
        pieces += [taken[hop * TOK : (hop + 1) * TOK], own[hop]]
    return jnp.concatenate(pieces, axis=0)


def window_sum(window, odd):
    part = [window[block * TOK : (block + 1) * TOK] for block in range(BLOCKS)]
    kept = [part[BACK - 2 * hop] for hop in range(HOPS + 1)]
    given = jnp.concatenate([part[BACK - 2 * hop - 1] for hop in range(HOPS)], axis=0).astype(jnp.bfloat16)
    taken = core_swapped(given).astype(jnp.float32).reshape(HOPS, TOK, -1)
    none = jnp.zeros((1,) + taken.shape[1:], taken.dtype)
    added = lax.select(odd, jnp.concatenate([none, taken]), jnp.concatenate([taken, none]))
    total = kept[0] + added[0]
    for hop in range(1, HOPS + 1):
        sent = (kept[hop] + added[hop]).astype(jnp.bfloat16)
        total = total + permuted(sent, -2 * hop).astype(jnp.float32)
    return total


def quad_partner(value, core, micro):
    chips, cores, reps = lax.axis_size("fsdp") // 2, 2, lax.axis_size("rep")
    moves = [
        ((chip * cores + here) * reps + rep, (chip * cores + (here ^ core)) * reps + (rep ^ micro))
        for chip in range(chips)
        for here in range(cores)
        for rep in range(reps)
    ]
    return lax.ppermute(value, ("fsdp", "rep"), moves)


def gathered_in_quad(value):
    return [value] + [quad_partner(value, core, micro) for core, micro in QUAD[1:]]


def inputs_in_quad(inputs, core, micro):
    chips, width = lax.axis_size("fsdp") // 2, inputs.shape[1] // 32
    pieces = inputs.reshape(TOK, chips, 2, 2, width).transpose(2, 3, 0, 1, 4).reshape(4, TOK, chips * width)
    own = [lax.dynamic_index_in_dim(pieces, 2 * (core ^ dc) + (micro ^ dm), 0, False) for dc, dm in QUAD]
    return [own[0]] + [quad_partner(piece, dc, dm) for piece, (dc, dm) in zip(own[1:], QUAD[1:])]


def shards(activations, query_rows, key_rows, out_grad, value_weight, doc_lengths):
    inputs = activations[0, 0]
    queries = query_rows[0, 0]
    keys = key_rows[0, 0]
    grads = out_grad[0, 0]
    weight_rows = value_weight[0]
    place = lax.axis_index("fsdp")
    core, micro = place % 2, lax.axis_index("rep")
    odd = core == 1
    info = jnp.concatenate([(place * TOK).reshape(1), doc_lengths[0]]).astype(jnp.int32)

    full_weight = lax.all_gather(weight_rows, "fsdp", axis=0, tiled=True)
    key_window = window_of(keys, odd)
    quad_inputs = jnp.concatenate(inputs_in_quad(inputs, core, micro), axis=0)

    probs, value_part = probs_and_value_grad(info, queries, grads, key_window)
    values = jnp.dot(inputs, full_weight, preferred_element_type=jnp.float32).astype(jnp.bfloat16)
    value_window = window_of(values, odd)
    value_grad = window_sum(value_part, odd).astype(jnp.bfloat16)

    quad_grads = jnp.concatenate(gathered_in_quad(value_grad), axis=0)
    weight_part = lax.dot_general(
        quad_inputs, quad_grads, (((0,), (0,)), ((), ())), preferred_element_type=jnp.float32
    ).astype(jnp.bfloat16)
    columns = [list(range(start, lax.axis_size("fsdp"), 2)) for start in range(2)]
    weight_half = lax.psum_scatter(
        weight_part, "fsdp", scatter_dimension=0, tiled=True, axis_index_groups=columns
    )
    other_half = lax.ppermute(weight_half, "rep", [(0, 1), (1, 0)])
    first = lax.select(micro == 0, weight_half, other_half)
    second = lax.select(micro == 0, other_half, weight_half)
    weight_grad = jnp.concatenate([first, second], axis=0)

    input_grad = lax.dot_general(
        value_grad, full_weight, (((1,), (1,)), ((), ())), preferred_element_type=jnp.float32
    ).astype(jnp.bfloat16)
    upstream = shifted(input_grad, "pipe", -1)

    query_out, key_part = query_and_key_grad(queries, grads, key_window, value_window, probs)
    key_grad = window_sum(key_part * SCALE, odd).astype(jnp.bfloat16)
    return (
        upstream[None, None],
        query_out[None, None],
        key_grad[None, None],
        weight_grad[None],
    )


def solution(mesh):
    tokens = P("pipe", "rep", "fsdp", None)
    weights = P("pipe", "fsdp", None)
    return jax.shard_map(
        shards,
        mesh=mesh,
        in_specs=(tokens, tokens, tokens, tokens, weights, P("rep", None)),
        out_specs=(tokens, tokens, tokens, weights),
        check_vma=False,
    )
```

```python
import jax
import jax.numpy as jnp
from jax import lax
from jax.experimental import pallas as pl
from jax.experimental.pallas import tpu as pltpu
from jax.sharding import PartitionSpec as P

HQ = 64
KV = 4
HD = 128
DOCS = 4
TOK = 128
LONGEST = 1024
BACK = LONGEST // TOK
BLOCKS = BACK + 1
HOPS = BACK // 2
WINDOW = BLOCKS * TOK
GROUP = HQ // KV
PAIRS = GROUP // 2
STEP_PAIRS = 8
STEPS = PAIRS // STEP_PAIRS
PART = 3 * TOK
PARTS = WINDOW // PART
SCALE = HD ** (-0.5)
LOG2E = 1.4426950408889634
MASKED = -1e30
NT = (((1,), (1,)), ((), ()))
NN = (((1,), (0,)), ((), ()))
TN = (((0,), (0,)), ((), ()))
CHIPS = 8
CORES = 2
REPS = 2
SLAB = 256


def dot(left, right, numbers):
    return lax.dot_general(left, right, numbers, preferred_element_type=jnp.float32)


def stacked(ref, pair):
    first = 2 * pair * HD
    return jnp.concatenate([ref[:, first : first + HD], ref[:, first + HD : first + 2 * HD]], axis=0)


def rows_of(block):
    return slice(block * TOK, (block + 1) * TOK)


def part_rows(part):
    return slice(part * PART, (part + 1) * PART)


def window_block(refs, block):
    hop, odd = divmod(BACK - block, 2)
    return refs[HOPS + 1][rows_of(hop), :] if odd else refs[hop][...]


def staggered(first, middle, second, finish=None):
    for pair in range(STEP_PAIRS + 1):
        for part in range(PARTS):
            if pair:
                second(pair - 1, part)
            if pair < STEP_PAIRS:
                first(pair, part)
        if middle and pair < STEP_PAIRS:
            middle(pair)
        if finish and pair:
            finish(pair - 1)


def probs_kernel(info_ref, query_ref, grad_ref, *refs):
    key_refs, (probs_ref, given_ref, kept_ref, bias_ref, total_ref, window_ref), score_refs = refs[:6], refs[-8:-2], refs[-2:]
    group, step = pl.program_id(0), pl.program_id(1)

    @pl.when((group == 0) & (step == 0))
    def _():
        begin = info_ref[0]
        query_pos = begin + lax.broadcasted_iota(jnp.int32, (1, TOK), 1)
        doc_start = jnp.zeros((1, TOK), jnp.int32)
        doc_end = 0
        for doc in range(DOCS):
            doc_end = doc_end + info_ref[1 + doc]
            doc_start = jnp.where(query_pos >= doc_end, doc_end, doc_start)
        key_pos = begin - BACK * TOK + lax.broadcasted_iota(jnp.int32, (WINDOW, TOK), 0)
        visible = (key_pos >= doc_start) & (key_pos <= query_pos)
        bias_ref[...] = jnp.where(visible, 0.0, MASKED)

    @pl.when(step == 0)
    def _():
        total_ref[...] = jnp.zeros_like(total_ref)
        for block in range(BLOCKS):
            window_ref[rows_of(block), :] = window_block(key_refs, block)

    queries = [stacked(query_ref, pair) for pair in range(STEP_PAIRS)]
    grads = [stacked(grad_ref, pair) for pair in range(STEP_PAIRS)]
    most, inverse = {}, {}

    def first(pair, part):
        rows = part_rows(part)
        bias = bias_ref[rows, :]
        scores = dot(window_ref[rows, :], queries[pair], NT) * (SCALE * LOG2E)
        scores = scores + jnp.concatenate([bias, bias], axis=1)
        score_refs[pair % 2][rows, :] = scores
        peak = jnp.max(scores.reshape(PART // 8, 8, 2 * TOK), axis=0)
        most[pair] = peak if part == 0 else jnp.maximum(most[pair], peak)

    def middle(pair):
        peak = jnp.max(most[pair], axis=0, keepdims=True)
        total = jnp.zeros((8, 2 * TOK), jnp.float32)
        for part in range(PARTS):
            numer = jnp.exp2(score_refs[pair % 2][part_rows(part), :] - peak)
            score_refs[pair % 2][part_rows(part), :] = numer
            total = total + jnp.sum(numer.reshape(PART // 8, 8, 2 * TOK), axis=0)
        total = jnp.sum(total, axis=0, keepdims=True)
        inverse[pair] = 1.0 / total

    def second(pair, part):
        rows = part_rows(part)
        probs = (score_refs[pair % 2][rows, :] * inverse[pair]).astype(jnp.bfloat16)
        probs_ref[pair, rows, :] = probs
        total_ref[rows, :] += dot(probs, grads[pair], NN)

    staggered(first, middle, second)

    @pl.when(step == STEPS - 1)
    def _():
        put_window(total_ref, given_ref, kept_ref, 1.0)


def put_window(total_ref, given_ref, kept_ref, factor):
    for block in range(BLOCKS):
        hop, odd = divmod(BACK - block, 2)
        if odd:
            given_ref[rows_of(hop), :] = (total_ref[rows_of(block), :] * factor).astype(jnp.bfloat16)
        else:
            kept_ref[rows_of(hop), :] = total_ref[rows_of(block), :] * factor


def grads_kernel(query_ref, grad_ref, probs_ref, *refs):
    key_refs, value_refs = refs[:6], refs[6:12]
    query_out_ref, given_ref, kept_ref, total_ref, window_ref, flip_ref = refs[-10:-4]
    dprobs_refs, dscores_refs = refs[-4:-2], refs[-2:]
    step = pl.program_id(1)

    @pl.when(step == 0)
    def _():
        total_ref[...] = jnp.zeros_like(total_ref)
        for block in range(BLOCKS):
            window_ref[rows_of(block), :] = window_block(value_refs, block)
            flip_ref[:, rows_of(block)] = window_block(key_refs, block).T

    queries = [stacked(query_ref, pair) for pair in range(STEP_PAIRS)]
    grads = [stacked(grad_ref, pair) for pair in range(STEP_PAIRS)]
    delta = {}

    def first(pair, part):
        rows = part_rows(part)
        dprobs = dot(window_ref[rows, :], grads[pair], NT)
        dprobs_refs[pair % 2][rows, :] = dprobs
        summed = jnp.sum((probs_ref[pair, rows, :].astype(jnp.float32) * dprobs).reshape(PART // 8, 8, 2 * TOK), axis=0)
        delta[pair] = summed if part == 0 else delta[pair] + summed

    def second(pair, part):
        rows = part_rows(part)
        if part == 0:
            delta[pair] = jnp.sum(delta[pair], axis=0, keepdims=True)
        probs = probs_ref[pair, rows, :].astype(jnp.float32)
        dscores = (probs * (dprobs_refs[pair % 2][rows, :] - delta[pair])).astype(jnp.bfloat16)
        dscores_refs[pair % 2][rows, :] = dscores
        total_ref[rows, :] += dot(dscores, queries[pair], NN)

    def finish(pair):
        flipped = dot(flip_ref[...], dscores_refs[pair % 2][...], NN) * SCALE
        for half in range(2):
            columns = slice((2 * pair + half) * HD, (2 * pair + half + 1) * HD)
            query_out_ref[:, columns] = flipped[:, half * TOK : (half + 1) * TOK].T.astype(jnp.bfloat16)

    staggered(first, None, second, finish)

    @pl.when(step == STEPS - 1)
    def _():
        put_window(total_ref, given_ref, kept_ref, SCALE)


def head_spec(first):
    return pl.BlockSpec((TOK, 2 * STEP_PAIRS * HD), lambda group, step: (0, (first + group) * STEPS + step))


def window_specs(first):
    return [pl.BlockSpec((rows, HD), lambda group, step: (0, first + group)) for rows in [TOK] * (HOPS + 1) + [HOPS * TOK]]


def sum_specs(first):
    return [pl.BlockSpec((rows, HD), lambda group, step: (0, first + group)) for rows in (HOPS * TOK, (HOPS + 1) * TOK)]


def probs_spec(first):
    return pl.BlockSpec((STEP_PAIRS, WINDOW, 2 * TOK), lambda group, step: ((first + group) * STEPS + step, 0, 0))


SUMS = [
    jax.ShapeDtypeStruct((HOPS * TOK, KV * HD), jnp.bfloat16),
    jax.ShapeDtypeStruct(((HOPS + 1) * TOK, KV * HD), jnp.float32),
]


def part_call(kernel, first, groups, operands, in_specs, out_shape, out_specs, scratch, earlier, cost):
    earlier = list(earlier or [])
    count = len(operands)
    return pl.pallas_call(
        kernel,
        grid=(groups, STEPS),
        in_specs=in_specs + [pl.BlockSpec(memory_space=pl.ANY)] * len(earlier),
        out_specs=out_specs,
        out_shape=out_shape,
        input_output_aliases={count + place: place for place in range(len(earlier))},
        scratch_shapes=scratch,
        compiler_params=pltpu.CompilerParams(vmem_limit_bytes=48 * 1024 * 1024),
        cost_estimate=cost,
    )(*operands, *earlier)


def probs_and_value_grad(first, groups, info, queries, grads, key_window, earlier=None):
    work = groups * GROUP * TOK * WINDOW
    return part_call(
        probs_kernel,
        first,
        groups,
        [info, queries, grads, *key_window],
        [pl.BlockSpec(memory_space=pltpu.SMEM), head_spec(first), head_spec(first)] + window_specs(first),
        [jax.ShapeDtypeStruct((HQ // 2, WINDOW, 2 * TOK), jnp.bfloat16)] + SUMS,
        [probs_spec(first)] + sum_specs(first),
        [
            pltpu.VMEM((WINDOW, TOK), jnp.float32),
            pltpu.VMEM((WINDOW, HD), jnp.float32),
            pltpu.VMEM((WINDOW, HD), jnp.bfloat16),
        ]
        + [pltpu.VMEM((WINDOW, 2 * TOK), jnp.float32)] * 2,
        earlier,
        pl.CostEstimate(flops=4 * work * HD, bytes_accessed=groups * (6 << 20), transcendentals=work),
    )


def query_and_key_grad(first, groups, queries, grads, probs, key_window, value_window, earlier=None):
    work = groups * GROUP * TOK * WINDOW
    return part_call(
        grads_kernel,
        first,
        groups,
        [queries, grads, probs, *key_window, *value_window],
        [head_spec(first), head_spec(first), probs_spec(first)] + window_specs(first) * 2,
        [jax.ShapeDtypeStruct((TOK, HQ * HD), jnp.bfloat16)] + SUMS,
        [head_spec(first)] + sum_specs(first),
        [
            pltpu.VMEM((WINDOW, HD), jnp.float32),
            pltpu.VMEM((WINDOW, HD), jnp.bfloat16),
            pltpu.VMEM((HD, WINDOW), jnp.bfloat16),
        ]
        + [pltpu.VMEM((WINDOW, 2 * TOK), jnp.float32)] * 2
        + [pltpu.VMEM((WINDOW, 2 * TOK), jnp.bfloat16)] * 2,
        earlier,
        pl.CostEstimate(flops=6 * work * HD, bytes_accessed=groups * (7 << 20), transcendentals=0),
    )


def quarter_columns(mine, offset, chip):
    start = (4 * chip + jnp.bitwise_xor(mine, offset)) * SLAB
    return pl.ds(pl.multiple_of(start, SLAB), SLAB)


def quarters_kernel(mine_ref, whole_ref, *quarter_refs):
    for offset, quarter_ref in enumerate(quarter_refs):
        for chip in range(CHIPS):
            quarter_ref[:, chip * SLAB : (chip + 1) * SLAB] = whole_ref[:, quarter_columns(mine_ref[0], offset, chip)]


def quarters_of(mine, whole):
    return pl.pallas_call(
        quarters_kernel,
        in_specs=[pl.BlockSpec(memory_space=pltpu.SMEM), pl.BlockSpec(memory_space=pltpu.VMEM)],
        out_specs=[pl.BlockSpec(memory_space=pltpu.VMEM)] * 4,
        out_shape=[jax.ShapeDtypeStruct((TOK, CHIPS * SLAB), jnp.bfloat16)] * 4,
        cost_estimate=pl.CostEstimate(flops=0, bytes_accessed=4 << 20, transcendentals=0),
    )(mine, whole)


def permuted(value, steps):
    count = lax.axis_size("fsdp")
    return lax.ppermute(value, "fsdp", [(source, (source + steps) % count) for source in range(count)])


def core_swapped(value):
    count = lax.axis_size("fsdp")
    return lax.ppermute(value, "fsdp", [(source, source ^ 1) for source in range(count)])


def quad_partner(value, offset, back=0):
    core, micro = offset // 2, offset % 2
    sections, places = lax.axis_size("pipe"), CHIPS * CORES
    moves = [
        (
            ((section * places) + place) * REPS + rep,
            (((section - back) * places) + (place ^ core)) * REPS + (rep ^ micro),
        )
        for section in range(back, sections)
        for place in range(places)
        for rep in range(REPS)
    ]
    return lax.ppermute(value, ("pipe", "fsdp", "rep"), moves)


def rounded(value):
    return value.astype(jnp.bfloat16)


def after(value, *earlier):
    return lax.optimization_barrier((value, earlier))[0]


def window_of(block, odd):
    own = [block]
    for hop in range(HOPS):
        own.append(permuted(own[-1], CORES))
    given = jnp.concatenate([lax.select(odd, own[hop + 1], own[hop]) for hop in range(HOPS)], axis=0)
    return own + [core_swapped(given)]


def chip_sums(given, kept, odd):
    taken = core_swapped(given).astype(jnp.float32).reshape(HOPS, TOK, -1)
    kept = kept.reshape(HOPS + 1, TOK, -1)
    none = jnp.zeros((1,) + taken.shape[1:], taken.dtype)
    kept = kept + lax.select(odd, jnp.concatenate([none, taken]), jnp.concatenate([taken, none]))
    return [kept[hop] for hop in range(HOPS)] + [rounded(kept[HOPS])]


def relayed_sum(sums, beside=()):
    total = sums[HOPS]
    for hop in reversed(range(HOPS)):
        total = after(total, *beside[HOPS - 1 - hop : HOPS - hop])
        total = rounded(sums[hop] + permuted(total, -CORES).astype(jnp.float32))
    return total


def shards(activations, query_rows, key_rows, out_grad, value_weight, doc_lengths):
    inputs = activations[0, 0]
    queries = query_rows[0, 0]
    keys = key_rows[0, 0]
    grads = out_grad[0, 0]
    weight_rows = value_weight[0]
    place = lax.axis_index("fsdp")
    core, micro = place % CORES, lax.axis_index("rep")
    odd = core == 1
    mine = (REPS * core + micro).reshape(1).astype(jnp.int32)
    info = jnp.concatenate([(place * TOK).reshape(1), doc_lengths[0]]).astype(jnp.int32)
    columns = [list(range(start, CHIPS * CORES, CORES)) for start in range(CORES)]

    weight = lax.all_gather(weight_rows, "fsdp", axis=0, tiled=True)
    quarters = quarters_of(mine, inputs)
    quad_inputs = [quarters[0]] + [quad_partner(quarters[offset], offset) for offset in range(1, 4)]
    key_window = window_of(after(keys, *quarters), odd)

    queries = after(queries, *quarters)
    probs, given, kept = probs_and_value_grad(0, KV, info, queries, grads, key_window)
    values = rounded(dot(inputs, after(weight, given), NN))
    value_window = window_of(values, odd)
    given = after(given, values, *quad_inputs[1:])
    value_grad = relayed_sum(chip_sums(given, kept, odd), value_window)

    moves = [(section, section - 1) for section in range(1, lax.axis_size("pipe"))]
    middle = weight.shape[0] * 3 // 4
    input_grads = [rounded(dot(value_grad, rows, NT)) for rows in (weight[:middle], weight[middle:])]
    upstreams = [lax.ppermute(part, "pipe", moves) for part in input_grads]
    upstream = jnp.concatenate(upstreams, axis=1)

    quad_grads = [value_grad] + [quad_partner(value_grad, offset) for offset in range(1, 4)]
    quad_grads = jnp.concatenate(after(quad_grads, *value_window[:HOPS], *input_grads), axis=0)
    weight_part = rounded(dot(jnp.concatenate(quad_inputs, axis=0), quad_grads, TN))
    weight_half = lax.psum_scatter(
        weight_part, "fsdp", scatter_dimension=0, tiled=True, axis_index_groups=columns
    )
    other_half = lax.ppermute(weight_half, "rep", [(0, 1), (1, 0)])
    first = lax.select(micro == 0, weight_half, other_half)
    second = lax.select(micro == 0, other_half, weight_half)
    weight_grad = jnp.concatenate([first, second], axis=0)

    queries = after(queries, weight_part)
    query_out, given, kept = query_and_key_grad(0, KV, queries, grads, probs, key_window, value_window)
    given = after(given, upstreams[0])
    key_grad = relayed_sum(chip_sums(given, kept, odd), [given] * (HOPS - 1) + [upstreams[1]])
    return (
        upstream[None, None],
        query_out[None, None],
        key_grad[None, None],
        weight_grad[None],
    )


def solution(mesh):
    tokens = P("pipe", "rep", "fsdp", None)
    weights = P("pipe", "fsdp", None)
    return jax.shard_map(
        shards,
        mesh=mesh,
        in_specs=(tokens, tokens, tokens, tokens, weights, P("rep", None)),
        out_specs=(tokens, tokens, tokens, weights),
        check_vma=False,
    )
```

```python
import jax
import jax.numpy as jnp
from jax import lax
from jax.experimental import pallas as pl
from jax.experimental.pallas import tpu as pltpu
from jax.sharding import PartitionSpec as P

HQ = 64
KV = 4
HD = 128
DOCS = 4
TOK = 128
LONGEST = 1024
BACK = LONGEST // TOK
BLOCKS = BACK + 1
HOPS = BACK // 2
WINDOW = BLOCKS * TOK
GROUP = HQ // KV
PAIRS = GROUP // 2
STEP_PAIRS = 8
STEPS = PAIRS // STEP_PAIRS
PART = 3 * TOK
PARTS = WINDOW // PART
SCALE = HD ** (-0.5)
LOG2E = 1.4426950408889634
MASKED = -1e30
NT = (((1,), (1,)), ((), ()))
NN = (((1,), (0,)), ((), ()))
TN = (((0,), (0,)), ((), ()))
CHIPS = 8
CORES = 2
REPS = 2
SLAB = 256


def dot(left, right, numbers):
    return lax.dot_general(left, right, numbers, preferred_element_type=jnp.float32)


def stacked(ref, pair):
    first = 2 * pair * HD
    return jnp.concatenate([ref[:, first : first + HD], ref[:, first + HD : first + 2 * HD]], axis=0)


def rows_of(block):
    return slice(block * TOK, (block + 1) * TOK)


def part_rows(part):
    return slice(part * PART, (part + 1) * PART)


def window_block(refs, block):
    hop, odd = divmod(BACK - block, 2)
    return refs[HOPS + 1][rows_of(hop), :] if odd else refs[hop][...]


def staggered(first, middle, second, finish=None):
    for pair in range(STEP_PAIRS + 1):
        for part in range(PARTS):
            if pair:
                second(pair - 1, part)
            if pair < STEP_PAIRS:
                first(pair, part)
        if middle and pair < STEP_PAIRS:
            middle(pair)
        if finish and pair:
            finish(pair - 1)


def probs_kernel(info_ref, query_ref, grad_ref, *refs):
    key_refs, (probs_ref, given_ref, kept_ref, bias_ref, total_ref, window_ref), score_refs = refs[:6], refs[-8:-2], refs[-2:]
    group, step = pl.program_id(0), pl.program_id(1)

    @pl.when((group == 0) & (step == 0))
    def _():
        begin = info_ref[0]
        query_pos = begin + lax.broadcasted_iota(jnp.int32, (1, TOK), 1)
        doc_start = jnp.zeros((1, TOK), jnp.int32)
        doc_end = 0
        for doc in range(DOCS):
            doc_end = doc_end + info_ref[1 + doc]
            doc_start = jnp.where(query_pos >= doc_end, doc_end, doc_start)
        key_pos = begin - BACK * TOK + lax.broadcasted_iota(jnp.int32, (WINDOW, TOK), 0)
        visible = (key_pos >= doc_start) & (key_pos <= query_pos)
        bias_ref[...] = jnp.where(visible, 0.0, MASKED)

    @pl.when(step == 0)
    def _():
        total_ref[...] = jnp.zeros_like(total_ref)
        for block in range(BLOCKS):
            window_ref[rows_of(block), :] = window_block(key_refs, block)

    queries = [stacked(query_ref, pair) for pair in range(STEP_PAIRS)]
    grads = [stacked(grad_ref, pair) for pair in range(STEP_PAIRS)]
    most, inverse = {}, {}

    def first(pair, part):
        rows = part_rows(part)
        bias = bias_ref[rows, :]
        scores = dot(window_ref[rows, :], queries[pair], NT) * (SCALE * LOG2E)
        scores = scores + jnp.concatenate([bias, bias], axis=1)
        score_refs[pair % 2][rows, :] = scores
        peak = jnp.max(scores.reshape(PART // 8, 8, 2 * TOK), axis=0)
        most[pair] = peak if part == 0 else jnp.maximum(most[pair], peak)

    def middle(pair):
        peak = jnp.max(most[pair], axis=0, keepdims=True)
        total = jnp.zeros((8, 2 * TOK), jnp.float32)
        for part in range(PARTS):
            numer = jnp.exp2(score_refs[pair % 2][part_rows(part), :] - peak)
            score_refs[pair % 2][part_rows(part), :] = numer
            total = total + jnp.sum(numer.reshape(PART // 8, 8, 2 * TOK), axis=0)
        total = jnp.sum(total, axis=0, keepdims=True)
        inverse[pair] = 1.0 / total

    def second(pair, part):
        rows = part_rows(part)
        probs = (score_refs[pair % 2][rows, :] * inverse[pair]).astype(jnp.bfloat16)
        probs_ref[pair, rows, :] = probs
        total_ref[rows, :] += dot(probs, grads[pair], NN)

    staggered(first, middle, second)

    @pl.when(step == STEPS - 1)
    def _():
        put_window(total_ref, given_ref, kept_ref, 1.0)


def put_window(total_ref, given_ref, kept_ref, factor):
    for block in range(BLOCKS):
        hop, odd = divmod(BACK - block, 2)
        if odd:
            given_ref[rows_of(hop), :] = (total_ref[rows_of(block), :] * factor).astype(jnp.bfloat16)
        else:
            kept_ref[rows_of(hop), :] = total_ref[rows_of(block), :] * factor


def grads_kernel(query_ref, grad_ref, probs_ref, *refs):
    key_refs, value_refs = refs[:6], refs[6:12]
    query_out_ref, given_ref, kept_ref, total_ref, window_ref, flip_ref = refs[-10:-4]
    dprobs_refs, dscores_refs = refs[-4:-2], refs[-2:]
    step = pl.program_id(1)

    @pl.when(step == 0)
    def _():
        total_ref[...] = jnp.zeros_like(total_ref)
        for block in range(BLOCKS):
            window_ref[rows_of(block), :] = window_block(value_refs, block)
            flip_ref[:, rows_of(block)] = window_block(key_refs, block).T

    queries = [stacked(query_ref, pair) for pair in range(STEP_PAIRS)]
    grads = [stacked(grad_ref, pair) for pair in range(STEP_PAIRS)]
    delta = {}

    def first(pair, part):
        rows = part_rows(part)
        dprobs = dot(window_ref[rows, :], grads[pair], NT)
        dprobs_refs[pair % 2][rows, :] = dprobs
        summed = jnp.sum((probs_ref[pair, rows, :].astype(jnp.float32) * dprobs).reshape(PART // 8, 8, 2 * TOK), axis=0)
        delta[pair] = summed if part == 0 else delta[pair] + summed

    def second(pair, part):
        rows = part_rows(part)
        if part == 0:
            delta[pair] = jnp.sum(delta[pair], axis=0, keepdims=True)
        probs = probs_ref[pair, rows, :].astype(jnp.float32)
        dscores = (probs * (dprobs_refs[pair % 2][rows, :] - delta[pair])).astype(jnp.bfloat16)
        dscores_refs[pair % 2][rows, :] = dscores
        total_ref[rows, :] += dot(dscores, queries[pair], NN)

    def finish(pair):
        flipped = dot(flip_ref[...], dscores_refs[pair % 2][...], NN) * SCALE
        for half in range(2):
            columns = slice((2 * pair + half) * HD, (2 * pair + half + 1) * HD)
            query_out_ref[:, columns] = flipped[:, half * TOK : (half + 1) * TOK].T.astype(jnp.bfloat16)

    staggered(first, None, second, finish)

    @pl.when(step == STEPS - 1)
    def _():
        put_window(total_ref, given_ref, kept_ref, SCALE)


def head_spec(first):
    return pl.BlockSpec((TOK, 2 * STEP_PAIRS * HD), lambda group, step: (0, (first + group) * STEPS + step))


def window_specs(first):
    return [pl.BlockSpec((rows, HD), lambda group, step: (0, first + group)) for rows in [TOK] * (HOPS + 1) + [HOPS * TOK]]


def sum_specs(first):
    return [pl.BlockSpec((rows, HD), lambda group, step: (0, first + group)) for rows in (HOPS * TOK, (HOPS + 1) * TOK)]


def probs_spec(first):
    return pl.BlockSpec((STEP_PAIRS, WINDOW, 2 * TOK), lambda group, step: ((first + group) * STEPS + step, 0, 0))


SUMS = [
    jax.ShapeDtypeStruct((HOPS * TOK, KV * HD), jnp.bfloat16),
    jax.ShapeDtypeStruct(((HOPS + 1) * TOK, KV * HD), jnp.float32),
]


def part_call(kernel, first, groups, operands, in_specs, out_shape, out_specs, scratch, earlier, cost):
    earlier = list(earlier or [])
    count = len(operands)
    return pl.pallas_call(
        kernel,
        grid=(groups, STEPS),
        in_specs=in_specs + [pl.BlockSpec(memory_space=pl.ANY)] * len(earlier),
        out_specs=out_specs,
        out_shape=out_shape,
        input_output_aliases={count + place: place for place in range(len(earlier))},
        scratch_shapes=scratch,
        compiler_params=pltpu.CompilerParams(vmem_limit_bytes=48 * 1024 * 1024),
        cost_estimate=cost,
    )(*operands, *earlier)


def probs_and_value_grad(first, groups, info, queries, grads, key_window, earlier=None):
    work = groups * GROUP * TOK * WINDOW
    return part_call(
        probs_kernel,
        first,
        groups,
        [info, queries, grads, *key_window],
        [pl.BlockSpec(memory_space=pltpu.SMEM), head_spec(first), head_spec(first)] + window_specs(first),
        [jax.ShapeDtypeStruct((HQ // 2, WINDOW, 2 * TOK), jnp.bfloat16)] + SUMS,
        [probs_spec(first)] + sum_specs(first),
        [
            pltpu.VMEM((WINDOW, TOK), jnp.float32),
            pltpu.VMEM((WINDOW, HD), jnp.float32),
            pltpu.VMEM((WINDOW, HD), jnp.bfloat16),
        ]
        + [pltpu.VMEM((WINDOW, 2 * TOK), jnp.float32)] * 2,
        earlier,
        pl.CostEstimate(flops=4 * work * HD, bytes_accessed=groups * (6 << 20), transcendentals=work),
    )


def query_and_key_grad(first, groups, queries, grads, probs, key_window, value_window, earlier=None):
    work = groups * GROUP * TOK * WINDOW
    return part_call(
        grads_kernel,
        first,
        groups,
        [queries, grads, probs, *key_window, *value_window],
        [head_spec(first), head_spec(first), probs_spec(first)] + window_specs(first) * 2,
        [jax.ShapeDtypeStruct((TOK, HQ * HD), jnp.bfloat16)] + SUMS,
        [head_spec(first)] + sum_specs(first),
        [
            pltpu.VMEM((WINDOW, HD), jnp.float32),
            pltpu.VMEM((WINDOW, HD), jnp.bfloat16),
            pltpu.VMEM((HD, WINDOW), jnp.bfloat16),
        ]
        + [pltpu.VMEM((WINDOW, 2 * TOK), jnp.float32)] * 2
        + [pltpu.VMEM((WINDOW, 2 * TOK), jnp.bfloat16)] * 2,
        earlier,
        pl.CostEstimate(flops=6 * work * HD, bytes_accessed=groups * (7 << 20), transcendentals=0),
    )


def quarter_columns(mine, offset, chip):
    start = (4 * chip + jnp.bitwise_xor(mine, offset)) * SLAB
    return pl.ds(pl.multiple_of(start, SLAB), SLAB)


def quarters_kernel(mine_ref, whole_ref, *quarter_refs):
    for offset, quarter_ref in enumerate(quarter_refs):
        for chip in range(CHIPS):
            quarter_ref[:, chip * SLAB : (chip + 1) * SLAB] = whole_ref[:, quarter_columns(mine_ref[0], offset, chip)]


def quarters_of(mine, whole):
    return pl.pallas_call(
        quarters_kernel,
        in_specs=[pl.BlockSpec(memory_space=pltpu.SMEM), pl.BlockSpec(memory_space=pltpu.VMEM)],
        out_specs=[pl.BlockSpec(memory_space=pltpu.VMEM)] * 4,
        out_shape=[jax.ShapeDtypeStruct((TOK, CHIPS * SLAB), jnp.bfloat16)] * 4,
        cost_estimate=pl.CostEstimate(flops=0, bytes_accessed=4 << 20, transcendentals=0),
    )(mine, whole)


def permuted(value, steps):
    count = lax.axis_size("fsdp")
    return lax.ppermute(value, "fsdp", [(source, (source + steps) % count) for source in range(count)])


def core_swapped(value):
    count = lax.axis_size("fsdp")
    return lax.ppermute(value, "fsdp", [(source, source ^ 1) for source in range(count)])


def quad_partner(value, offset, back=0):
    core, micro = offset // 2, offset % 2
    sections, places = lax.axis_size("pipe"), CHIPS * CORES
    moves = [
        (
            ((section * places) + place) * REPS + rep,
            (((section - back) * places) + (place ^ core)) * REPS + (rep ^ micro),
        )
        for section in range(back, sections)
        for place in range(places)
        for rep in range(REPS)
    ]
    return lax.ppermute(value, ("pipe", "fsdp", "rep"), moves)


def rounded(value):
    return value.astype(jnp.bfloat16)


def after(value, *earlier):
    return lax.optimization_barrier((value, earlier))[0]


def window_of(block, odd, beside=()):
    own = [block]
    for hop in range(HOPS):
        own.append(permuted(own[-1], CORES))
        if hop == 0 and beside:
            own[-1] = after(own[-1], *beside)
    given = jnp.concatenate([lax.select(odd, own[hop + 1], own[hop]) for hop in range(HOPS)], axis=0)
    return own + [core_swapped(given)]


def chip_sums(given, kept, odd):
    taken = core_swapped(given).astype(jnp.float32).reshape(HOPS, TOK, -1)
    kept = kept.reshape(HOPS + 1, TOK, -1)
    none = jnp.zeros((1,) + taken.shape[1:], taken.dtype)
    kept = kept + lax.select(odd, jnp.concatenate([none, taken]), jnp.concatenate([taken, none]))
    return [kept[hop] for hop in range(HOPS)] + [rounded(kept[HOPS])]


def relayed_sum(sums, beside=()):
    total = sums[HOPS]
    for step in range(HOPS):
        arrived = after(permuted(total, -CORES), *beside[step : step + 1])
        total = rounded(sums[HOPS - 1 - step] + arrived.astype(jnp.float32))
    return total


def shards(activations, query_rows, key_rows, out_grad, value_weight, doc_lengths):
    inputs = activations[0, 0]
    queries = query_rows[0, 0]
    keys = key_rows[0, 0]
    grads = out_grad[0, 0]
    weight_rows = value_weight[0]
    place = lax.axis_index("fsdp")
    core, micro = place % CORES, lax.axis_index("rep")
    odd = core == 1
    mine = (REPS * core + micro).reshape(1).astype(jnp.int32)
    info = jnp.concatenate([(place * TOK).reshape(1), doc_lengths[0]]).astype(jnp.int32)
    columns = [list(range(start, CHIPS * CORES, CORES)) for start in range(CORES)]

    weight = lax.all_gather(weight_rows, "fsdp", axis=0, tiled=True)
    quarters = quarters_of(mine, inputs)
    quad_inputs = [quarters[0]] + [quad_partner(quarters[offset], offset) for offset in range(1, 4)]
    key_window = window_of(keys, odd, quarters)

    probs, given, kept = probs_and_value_grad(0, KV, info, queries, grads, key_window)
    sums = chip_sums(after(given, *quad_inputs[1:]), kept, odd)
    values = rounded(dot(inputs, after(weight, sums[HOPS]), NN))
    value_window = window_of(values, odd)
    value_grad = relayed_sum(sums, [values, *value_window[1:HOPS]])

    moves = [(section, section - 1) for section in range(1, lax.axis_size("pipe"))]
    input_grad = rounded(dot(value_grad, weight, NT))
    upstream = lax.ppermute(input_grad, "pipe", moves)

    quad_grads = [value_grad] + [quad_partner(value_grad, offset) for offset in range(1, 4)]
    quad_grads = jnp.concatenate(after(quad_grads, *value_window, input_grad), axis=0)
    weight_part = rounded(dot(jnp.concatenate(quad_inputs, axis=0), quad_grads, TN))
    weight_half = lax.psum_scatter(
        weight_part, "fsdp", scatter_dimension=0, tiled=True, axis_index_groups=columns
    )
    other_half = lax.ppermute(weight_half, "rep", [(0, 1), (1, 0)])
    first = lax.select(micro == 0, weight_half, other_half)
    second = lax.select(micro == 0, other_half, weight_half)
    weight_grad = jnp.concatenate([first, second], axis=0)

    value_window[0] = after(value_window[0], weight_part)
    query_out, given, kept = query_and_key_grad(0, KV, queries, grads, probs, key_window, value_window)
    key_grad = relayed_sum(chip_sums(given, kept, odd), [given, upstream])
    return (
        upstream[None, None],
        query_out[None, None],
        key_grad[None, None],
        weight_grad[None],
    )


def solution(mesh):
    tokens = P("pipe", "rep", "fsdp", None)
    weights = P("pipe", "fsdp", None)
    return jax.shard_map(
        shards,
        mesh=mesh,
        in_specs=(tokens, tokens, tokens, tokens, weights, P("rep", None)),
        out_specs=(tokens, tokens, tokens, weights),
        check_vma=False,
    )
```

```python
import jax
import jax.numpy as jnp
from jax import lax
from jax.experimental import pallas as pl
from jax.experimental.pallas import tpu as pltpu
from jax.sharding import PartitionSpec as P

HQ = 64
KV = 4
HD = 128
DOCS = 4
TOK = 128
LONGEST = 1024
BACK = LONGEST // TOK
BLOCKS = BACK + 1
HOPS = BACK // 2
WINDOW = BLOCKS * TOK
GROUP = HQ // KV
PAIRS = GROUP // 2
STEP_PAIRS = 8
STEPS = PAIRS // STEP_PAIRS
PART = 3 * TOK
PARTS = WINDOW // PART
SCALE = HD ** (-0.5)
LOG2E = 1.4426950408889634
MASKED = -1e30
NT = (((1,), (1,)), ((), ()))
NN = (((1,), (0,)), ((), ()))
TN = (((0,), (0,)), ((), ()))
CHIPS = 8
CORES = 2
REPS = 2
SLAB = 256


def dot(left, right, numbers):
    return lax.dot_general(left, right, numbers, preferred_element_type=jnp.float32)


def stacked(ref, pair):
    first = 2 * pair * HD
    return jnp.concatenate([ref[:, first : first + HD], ref[:, first + HD : first + 2 * HD]], axis=0)


def rows_of(block):
    return slice(block * TOK, (block + 1) * TOK)


def part_rows(part):
    return slice(part * PART, (part + 1) * PART)


def window_block(refs, block):
    hop, odd = divmod(BACK - block, 2)
    return refs[HOPS + 1][rows_of(hop), :] if odd else refs[hop][...]


def staggered(first, middle, second, finish=None):
    for pair in range(STEP_PAIRS + 1):
        for part in range(PARTS):
            if pair:
                second(pair - 1, part)
            if pair < STEP_PAIRS:
                first(pair, part)
        if middle and pair < STEP_PAIRS:
            middle(pair)
        if finish and pair:
            finish(pair - 1)


def probs_kernel(info_ref, query_ref, grad_ref, *refs):
    key_refs, (probs_ref, given_ref, kept_ref, bias_ref, total_ref, window_ref), score_refs = refs[:6], refs[-8:-2], refs[-2:]
    group, step = pl.program_id(0), pl.program_id(1)

    @pl.when((group == 0) & (step == 0))
    def _():
        begin = info_ref[0]
        query_pos = begin + lax.broadcasted_iota(jnp.int32, (1, TOK), 1)
        doc_start = jnp.zeros((1, TOK), jnp.int32)
        doc_end = 0
        for doc in range(DOCS):
            doc_end = doc_end + info_ref[1 + doc]
            doc_start = jnp.where(query_pos >= doc_end, doc_end, doc_start)
        key_pos = begin - BACK * TOK + lax.broadcasted_iota(jnp.int32, (WINDOW, TOK), 0)
        visible = (key_pos >= doc_start) & (key_pos <= query_pos)
        bias_ref[...] = jnp.where(visible, 0.0, MASKED)

    @pl.when(step == 0)
    def _():
        total_ref[...] = jnp.zeros_like(total_ref)
        for block in range(BLOCKS):
            window_ref[rows_of(block), :] = window_block(key_refs, block)

    queries = [stacked(query_ref, pair) for pair in range(STEP_PAIRS)]
    grads = [stacked(grad_ref, pair) for pair in range(STEP_PAIRS)]
    most, inverse = {}, {}

    def first(pair, part):
        rows = part_rows(part)
        bias = bias_ref[rows, :]
        scores = dot(window_ref[rows, :], queries[pair], NT) * (SCALE * LOG2E)
        scores = scores + jnp.concatenate([bias, bias], axis=1)
        score_refs[pair % 2][rows, :] = scores
        peak = jnp.max(scores.reshape(PART // 8, 8, 2 * TOK), axis=0)
        most[pair] = peak if part == 0 else jnp.maximum(most[pair], peak)

    def middle(pair):
        peak = jnp.max(most[pair], axis=0, keepdims=True)
        total = jnp.zeros((8, 2 * TOK), jnp.float32)
        for part in range(PARTS):
            numer = jnp.exp2(score_refs[pair % 2][part_rows(part), :] - peak)
            score_refs[pair % 2][part_rows(part), :] = numer
            total = total + jnp.sum(numer.reshape(PART // 8, 8, 2 * TOK), axis=0)
        total = jnp.sum(total, axis=0, keepdims=True)
        inverse[pair] = 1.0 / total

    def second(pair, part):
        rows = part_rows(part)
        probs = (score_refs[pair % 2][rows, :] * inverse[pair]).astype(jnp.bfloat16)
        probs_ref[pair, rows, :] = probs
        total_ref[rows, :] += dot(probs, grads[pair], NN)

    staggered(first, middle, second)

    @pl.when(step == STEPS - 1)
    def _():
        put_window(total_ref, given_ref, kept_ref, 1.0)


def put_window(total_ref, given_ref, kept_ref, factor):
    for block in range(BLOCKS):
        hop, odd = divmod(BACK - block, 2)
        if odd:
            given_ref[rows_of(hop), :] = (total_ref[rows_of(block), :] * factor).astype(jnp.bfloat16)
        else:
            kept_ref[rows_of(hop), :] = total_ref[rows_of(block), :] * factor


def grads_kernel(query_ref, grad_ref, probs_ref, *refs):
    key_refs, value_refs = refs[:6], refs[6:12]
    query_out_ref, given_ref, kept_ref, total_ref, window_ref, flip_ref = refs[-10:-4]
    dprobs_refs, dscores_refs = refs[-4:-2], refs[-2:]
    step = pl.program_id(1)

    @pl.when(step == 0)
    def _():
        total_ref[...] = jnp.zeros_like(total_ref)
        for block in range(BLOCKS):
            window_ref[rows_of(block), :] = window_block(value_refs, block)
            flip_ref[:, rows_of(block)] = window_block(key_refs, block).T

    queries = [stacked(query_ref, pair) for pair in range(STEP_PAIRS)]
    grads = [stacked(grad_ref, pair) for pair in range(STEP_PAIRS)]
    delta = {}

    def first(pair, part):
        rows = part_rows(part)
        dprobs = dot(window_ref[rows, :], grads[pair], NT)
        dprobs_refs[pair % 2][rows, :] = dprobs
        summed = jnp.sum((probs_ref[pair, rows, :].astype(jnp.float32) * dprobs).reshape(PART // 8, 8, 2 * TOK), axis=0)
        delta[pair] = summed if part == 0 else delta[pair] + summed

    def second(pair, part):
        rows = part_rows(part)
        if part == 0:
            delta[pair] = jnp.sum(delta[pair], axis=0, keepdims=True)
        probs = probs_ref[pair, rows, :].astype(jnp.float32)
        dscores = (probs * (dprobs_refs[pair % 2][rows, :] - delta[pair])).astype(jnp.bfloat16)
        dscores_refs[pair % 2][rows, :] = dscores
        total_ref[rows, :] += dot(dscores, queries[pair], NN)

    def finish(pair):
        flipped = dot(flip_ref[...], dscores_refs[pair % 2][...], NN) * SCALE
        for half in range(2):
            columns = slice((2 * pair + half) * HD, (2 * pair + half + 1) * HD)
            query_out_ref[:, columns] = flipped[:, half * TOK : (half + 1) * TOK].T.astype(jnp.bfloat16)

    staggered(first, None, second, finish)

    @pl.when(step == STEPS - 1)
    def _():
        put_window(total_ref, given_ref, kept_ref, SCALE)


def head_spec(first):
    return pl.BlockSpec((TOK, 2 * STEP_PAIRS * HD), lambda group, step: (0, (first + group) * STEPS + step))


def window_specs(first):
    return [pl.BlockSpec((rows, HD), lambda group, step: (0, first + group)) for rows in [TOK] * (HOPS + 1) + [HOPS * TOK]]


def sum_specs(first):
    return [pl.BlockSpec((rows, HD), lambda group, step: (0, first + group)) for rows in (HOPS * TOK, (HOPS + 1) * TOK)]


def probs_spec(first):
    return pl.BlockSpec((STEP_PAIRS, WINDOW, 2 * TOK), lambda group, step: ((first + group) * STEPS + step, 0, 0))


SUMS = [
    jax.ShapeDtypeStruct((HOPS * TOK, KV * HD), jnp.bfloat16),
    jax.ShapeDtypeStruct(((HOPS + 1) * TOK, KV * HD), jnp.float32),
]


def part_call(kernel, first, groups, operands, in_specs, out_shape, out_specs, scratch, earlier, cost):
    earlier = list(earlier or [])
    count = len(operands)
    return pl.pallas_call(
        kernel,
        grid=(groups, STEPS),
        in_specs=in_specs + [pl.BlockSpec(memory_space=pl.ANY)] * len(earlier),
        out_specs=out_specs,
        out_shape=out_shape,
        input_output_aliases={count + place: place for place in range(len(earlier))},
        scratch_shapes=scratch,
        compiler_params=pltpu.CompilerParams(vmem_limit_bytes=48 * 1024 * 1024),
        cost_estimate=cost,
    )(*operands, *earlier)


def probs_and_value_grad(first, groups, info, queries, grads, key_window, earlier=None):
    work = groups * GROUP * TOK * WINDOW
    return part_call(
        probs_kernel,
        first,
        groups,
        [info, queries, grads, *key_window],
        [pl.BlockSpec(memory_space=pltpu.SMEM), head_spec(first), head_spec(first)] + window_specs(first),
        [jax.ShapeDtypeStruct((HQ // 2, WINDOW, 2 * TOK), jnp.bfloat16)] + SUMS,
        [probs_spec(first)] + sum_specs(first),
        [
            pltpu.VMEM((WINDOW, TOK), jnp.float32),
            pltpu.VMEM((WINDOW, HD), jnp.float32),
            pltpu.VMEM((WINDOW, HD), jnp.bfloat16),
        ]
        + [pltpu.VMEM((WINDOW, 2 * TOK), jnp.float32)] * 2,
        earlier,
        pl.CostEstimate(flops=4 * work * HD, bytes_accessed=groups * (6 << 20), transcendentals=work),
    )


def query_and_key_grad(first, groups, queries, grads, probs, key_window, value_window, earlier=None):
    work = groups * GROUP * TOK * WINDOW
    return part_call(
        grads_kernel,
        first,
        groups,
        [queries, grads, probs, *key_window, *value_window],
        [head_spec(first), head_spec(first), probs_spec(first)] + window_specs(first) * 2,
        [jax.ShapeDtypeStruct((TOK, HQ * HD), jnp.bfloat16)] + SUMS,
        [head_spec(first)] + sum_specs(first),
        [
            pltpu.VMEM((WINDOW, HD), jnp.float32),
            pltpu.VMEM((WINDOW, HD), jnp.bfloat16),
            pltpu.VMEM((HD, WINDOW), jnp.bfloat16),
        ]
        + [pltpu.VMEM((WINDOW, 2 * TOK), jnp.float32)] * 2
        + [pltpu.VMEM((WINDOW, 2 * TOK), jnp.bfloat16)] * 2,
        earlier,
        pl.CostEstimate(flops=0, bytes_accessed=0, transcendentals=0),
    )


def quarter_columns(mine, offset, chip):
    start = (4 * chip + jnp.bitwise_xor(mine, offset)) * SLAB
    return pl.ds(pl.multiple_of(start, SLAB), SLAB)


def quarters_kernel(mine_ref, whole_ref, *quarter_refs):
    for offset, quarter_ref in enumerate(quarter_refs):
        for chip in range(CHIPS):
            quarter_ref[:, chip * SLAB : (chip + 1) * SLAB] = whole_ref[:, quarter_columns(mine_ref[0], offset, chip)]


def quarters_of(mine, whole):
    return pl.pallas_call(
        quarters_kernel,
        in_specs=[pl.BlockSpec(memory_space=pltpu.SMEM), pl.BlockSpec(memory_space=pltpu.VMEM)],
        out_specs=[pl.BlockSpec(memory_space=pltpu.VMEM)] * 4,
        out_shape=[jax.ShapeDtypeStruct((TOK, CHIPS * SLAB), jnp.bfloat16)] * 4,
        cost_estimate=pl.CostEstimate(flops=0, bytes_accessed=4 << 20, transcendentals=0),
    )(mine, whole)


def permuted(value, steps):
    count = lax.axis_size("fsdp")
    return lax.ppermute(value, "fsdp", [(source, (source + steps) % count) for source in range(count)])


def core_swapped(value):
    count = lax.axis_size("fsdp")
    return lax.ppermute(value, "fsdp", [(source, source ^ 1) for source in range(count)])


def quad_partner(value, offset, back=0):
    core, micro = offset // 2, offset % 2
    sections, places = lax.axis_size("pipe"), CHIPS * CORES
    moves = [
        (
            ((section * places) + place) * REPS + rep,
            (((section - back) * places) + (place ^ core)) * REPS + (rep ^ micro),
        )
        for section in range(back, sections)
        for place in range(places)
        for rep in range(REPS)
    ]
    return lax.ppermute(value, ("pipe", "fsdp", "rep"), moves)


def rounded(value):
    return value.astype(jnp.bfloat16)


def after(value, *earlier):
    return lax.optimization_barrier((value, earlier))[0]


def window_of(block, odd, beside=()):
    own = [block]
    for hop in range(HOPS):
        own.append(permuted(own[-1], CORES))
        if hop == 0 and beside:
            own[-1] = after(own[-1], *beside)
    given = jnp.concatenate([lax.select(odd, own[hop + 1], own[hop]) for hop in range(HOPS)], axis=0)
    return own + [core_swapped(given)]


def chip_sums(given, kept, odd):
    taken = core_swapped(given).astype(jnp.float32).reshape(HOPS, TOK, -1)
    kept = kept.reshape(HOPS + 1, TOK, -1)
    none = jnp.zeros((1,) + taken.shape[1:], taken.dtype)
    kept = kept + lax.select(odd, jnp.concatenate([none, taken]), jnp.concatenate([taken, none]))
    return [kept[hop] for hop in range(HOPS)] + [rounded(kept[HOPS])]


def relayed_sum(sums, beside=()):
    total = sums[HOPS]
    for step in range(HOPS):
        arrived = after(permuted(total, -CORES), *beside[step : step + 1])
        total = rounded(sums[HOPS - 1 - step] + arrived.astype(jnp.float32))
    return total


def shards(activations, query_rows, key_rows, out_grad, value_weight, doc_lengths):
    inputs = activations[0, 0]
    queries = query_rows[0, 0]
    keys = key_rows[0, 0]
    grads = out_grad[0, 0]
    weight_rows = value_weight[0]
    place = lax.axis_index("fsdp")
    core, micro = place % CORES, lax.axis_index("rep")
    odd = core == 1
    mine = (REPS * core + micro).reshape(1).astype(jnp.int32)
    info = jnp.concatenate([(place * TOK).reshape(1), doc_lengths[0]]).astype(jnp.int32)
    columns = [list(range(start, CHIPS * CORES, CORES)) for start in range(CORES)]

    weight = lax.all_gather(weight_rows, "fsdp", axis=0, tiled=True)
    quarters = quarters_of(mine, inputs)
    quad_inputs = [quarters[0]] + [quad_partner(quarters[offset], offset) for offset in range(1, 4)]
    key_window = window_of(keys, odd, quarters)

    probs, given, kept = probs_and_value_grad(0, KV, info, queries, grads, key_window)
    sums = chip_sums(after(given, *quad_inputs[1:]), kept, odd)
    values = rounded(dot(inputs, after(weight, sums[HOPS]), NN))
    value_window = window_of(values, odd)
    value_grad = relayed_sum(sums, [values, *value_window[1:HOPS]])

    moves = [(section, section - 1) for section in range(1, lax.axis_size("pipe"))]
    middle = weight.shape[0] * 7 // 8
    input_grads = [rounded(dot(value_grad, rows, NT)) for rows in (weight[:middle], weight[middle:])]
    upstreams = [lax.ppermute(part, "pipe", moves) for part in input_grads]
    upstream = jnp.concatenate(upstreams, axis=1)

    quad_grads = [value_grad] + [quad_partner(value_grad, offset) for offset in range(1, 4)]
    quad_grads = jnp.concatenate(after(quad_grads, *value_window, *input_grads), axis=0)
    weight_part = rounded(dot(jnp.concatenate(quad_inputs, axis=0), quad_grads, TN))
    weight_half = lax.psum_scatter(
        weight_part, "fsdp", scatter_dimension=0, tiled=True, axis_index_groups=columns
    )
    other_half = lax.ppermute(weight_half, "rep", [(0, 1), (1, 0)])
    first = lax.select(micro == 0, weight_half, other_half)
    second = lax.select(micro == 0, other_half, weight_half)
    weight_grad = jnp.concatenate([first, second], axis=0)

    value_window[0] = after(value_window[0], weight_part)
    query_out, given, kept = query_and_key_grad(0, KV, queries, grads, probs, key_window, value_window)
    sums = chip_sums(after(given, upstreams[0]), kept, odd)
    key_grad = relayed_sum(sums, [given, upstreams[1], (upstream, weight_half)])
    return (
        upstream[None, None],
        query_out[None, None],
        key_grad[None, None],
        weight_grad[None],
    )


def solution(mesh):
    tokens = P("pipe", "rep", "fsdp", None)
    weights = P("pipe", "fsdp", None)
    return jax.shard_map(
        shards,
        mesh=mesh,
        in_specs=(tokens, tokens, tokens, tokens, weights, P("rep", None)),
        out_specs=(tokens, tokens, tokens, weights),
        check_vma=False,
    )
```

```python
import jax
import jax.numpy as jnp
from jax import lax
from jax.experimental import pallas as pl
from jax.experimental.pallas import tpu as pltpu
from jax.sharding import PartitionSpec as P

HQ = 64
KV = 4
HD = 128
DOCS = 4
TOK = 128
LONGEST = 1024
BACK = LONGEST // TOK
BLOCKS = BACK + 1
HOPS = BACK // 2
WINDOW = BLOCKS * TOK
GROUP = HQ // KV
PAIRS = GROUP // 2
STEP_PAIRS = 8
STEPS = PAIRS // STEP_PAIRS
PART = 3 * TOK
PARTS = WINDOW // PART
SCALE = HD ** (-0.5)
LOG2E = 1.4426950408889634
MASKED = -1e30
NT = (((1,), (1,)), ((), ()))
NN = (((1,), (0,)), ((), ()))
TN = (((0,), (0,)), ((), ()))
CHIPS = 8
CORES = 2
REPS = 2
SLAB = 256


def dot(left, right, numbers):
    return lax.dot_general(left, right, numbers, preferred_element_type=jnp.float32)


def stacked(ref, pair):
    first = 2 * pair * HD
    return jnp.concatenate([ref[:, first : first + HD], ref[:, first + HD : first + 2 * HD]], axis=0)


def rows_of(block):
    return slice(block * TOK, (block + 1) * TOK)


def part_rows(part):
    return slice(part * PART, (part + 1) * PART)


def window_block(refs, block):
    hop, odd = divmod(BACK - block, 2)
    return refs[HOPS + 1][rows_of(hop), :] if odd else refs[hop][...]


def staggered(first, middle, second, finish=None):
    for pair in range(STEP_PAIRS + 1):
        for part in range(PARTS):
            if pair:
                second(pair - 1, part)
            if pair < STEP_PAIRS:
                first(pair, part)
        if middle and pair < STEP_PAIRS:
            middle(pair)
        if finish and pair:
            finish(pair - 1)


def probs_kernel(info_ref, query_ref, grad_ref, *refs):
    key_refs, (probs_ref, given_ref, kept_ref, bias_ref, total_ref, window_ref), score_refs = refs[:6], refs[-8:-2], refs[-2:]
    group, step = pl.program_id(0), pl.program_id(1)

    @pl.when((group == 0) & (step == 0))
    def _():
        begin = info_ref[0]
        query_pos = begin + lax.broadcasted_iota(jnp.int32, (1, TOK), 1)
        doc_start = jnp.zeros((1, TOK), jnp.int32)
        doc_end = 0
        for doc in range(DOCS):
            doc_end = doc_end + info_ref[1 + doc]
            doc_start = jnp.where(query_pos >= doc_end, doc_end, doc_start)
        key_pos = begin - BACK * TOK + lax.broadcasted_iota(jnp.int32, (WINDOW, TOK), 0)
        visible = (key_pos >= doc_start) & (key_pos <= query_pos)
        bias_ref[...] = jnp.where(visible, 0.0, MASKED)

    @pl.when(step == 0)
    def _():
        total_ref[...] = jnp.zeros_like(total_ref)
        for block in range(BLOCKS):
            window_ref[rows_of(block), :] = window_block(key_refs, block)

    queries = [stacked(query_ref, pair) for pair in range(STEP_PAIRS)]
    grads = [stacked(grad_ref, pair) for pair in range(STEP_PAIRS)]
    most, inverse = {}, {}

    def first(pair, part):
        rows = part_rows(part)
        bias = bias_ref[rows, :]
        scores = dot(window_ref[rows, :], queries[pair], NT) * (SCALE * LOG2E)
        scores = scores + jnp.concatenate([bias, bias], axis=1)
        score_refs[pair % 2][rows, :] = scores
        peak = jnp.max(scores.reshape(PART // 8, 8, 2 * TOK), axis=0)
        most[pair] = peak if part == 0 else jnp.maximum(most[pair], peak)

    def middle(pair):
        peak = jnp.max(most[pair], axis=0, keepdims=True)
        total = jnp.zeros((8, 2 * TOK), jnp.float32)
        for part in range(PARTS):
            numer = jnp.exp2(score_refs[pair % 2][part_rows(part), :] - peak)
            score_refs[pair % 2][part_rows(part), :] = numer
            total = total + jnp.sum(numer.reshape(PART // 8, 8, 2 * TOK), axis=0)
        total = jnp.sum(total, axis=0, keepdims=True)
        inverse[pair] = 1.0 / total

    def second(pair, part):
        rows = part_rows(part)
        probs = (score_refs[pair % 2][rows, :] * inverse[pair]).astype(jnp.bfloat16)
        probs_ref[pair, rows, :] = probs
        total_ref[rows, :] += dot(probs, grads[pair], NN)

    staggered(first, middle, second)

    @pl.when(step == STEPS - 1)
    def _():
        put_window(total_ref, given_ref, kept_ref, 1.0)


def put_window(total_ref, given_ref, kept_ref, factor):
    for block in range(BLOCKS):
        hop, odd = divmod(BACK - block, 2)
        if odd:
            given_ref[rows_of(hop), :] = (total_ref[rows_of(block), :] * factor).astype(jnp.bfloat16)
        else:
            kept_ref[rows_of(hop), :] = total_ref[rows_of(block), :] * factor


def grads_kernel(query_ref, grad_ref, probs_ref, *refs):
    key_refs, value_refs = refs[:6], refs[6:12]
    query_out_ref, given_ref, kept_ref, total_ref, window_ref, flip_ref = refs[-10:-4]
    dprobs_refs, dscores_refs = refs[-4:-2], refs[-2:]
    step = pl.program_id(1)

    @pl.when(step == 0)
    def _():
        total_ref[...] = jnp.zeros_like(total_ref)
        for block in range(BLOCKS):
            window_ref[rows_of(block), :] = window_block(value_refs, block)
            flip_ref[:, rows_of(block)] = window_block(key_refs, block).T

    queries = [stacked(query_ref, pair) for pair in range(STEP_PAIRS)]
    grads = [stacked(grad_ref, pair) for pair in range(STEP_PAIRS)]
    delta = {}

    def first(pair, part):
        rows = part_rows(part)
        dprobs = dot(window_ref[rows, :], grads[pair], NT)
        dprobs_refs[pair % 2][rows, :] = dprobs
        summed = jnp.sum((probs_ref[pair, rows, :].astype(jnp.float32) * dprobs).reshape(PART // 8, 8, 2 * TOK), axis=0)
        delta[pair] = summed if part == 0 else delta[pair] + summed

    def second(pair, part):
        rows = part_rows(part)
        if part == 0:
            delta[pair] = jnp.sum(delta[pair], axis=0, keepdims=True)
        probs = probs_ref[pair, rows, :].astype(jnp.float32)
        dscores = (probs * (dprobs_refs[pair % 2][rows, :] - delta[pair])).astype(jnp.bfloat16)
        dscores_refs[pair % 2][rows, :] = dscores
        total_ref[rows, :] += dot(dscores, queries[pair], NN)

    def finish(pair):
        flipped = dot(flip_ref[...], dscores_refs[pair % 2][...], NN) * SCALE
        for half in range(2):
            columns = slice((2 * pair + half) * HD, (2 * pair + half + 1) * HD)
            query_out_ref[:, columns] = flipped[:, half * TOK : (half + 1) * TOK].T.astype(jnp.bfloat16)

    staggered(first, None, second, finish)

    @pl.when(step == STEPS - 1)
    def _():
        put_window(total_ref, given_ref, kept_ref, SCALE)


def head_spec(first):
    return pl.BlockSpec((TOK, 2 * STEP_PAIRS * HD), lambda group, step: (0, (first + group) * STEPS + step))


def window_specs(first):
    return [pl.BlockSpec((rows, HD), lambda group, step: (0, first + group)) for rows in [TOK] * (HOPS + 1) + [HOPS * TOK]]


def sum_specs(first):
    return [pl.BlockSpec((rows, HD), lambda group, step: (0, first + group)) for rows in (HOPS * TOK, (HOPS + 1) * TOK)]


def probs_spec(first):
    return pl.BlockSpec((STEP_PAIRS, WINDOW, 2 * TOK), lambda group, step: ((first + group) * STEPS + step, 0, 0))


SUMS = [
    jax.ShapeDtypeStruct((HOPS * TOK, KV * HD), jnp.bfloat16),
    jax.ShapeDtypeStruct(((HOPS + 1) * TOK, KV * HD), jnp.float32),
]


def part_call(kernel, first, groups, operands, in_specs, out_shape, out_specs, scratch, earlier, cost):
    earlier = list(earlier or [])
    count = len(operands)
    return pl.pallas_call(
        kernel,
        grid=(groups, STEPS),
        in_specs=in_specs + [pl.BlockSpec(memory_space=pl.ANY)] * len(earlier),
        out_specs=out_specs,
        out_shape=out_shape,
        input_output_aliases={count + place: place for place in range(len(earlier))},
        scratch_shapes=scratch,
        compiler_params=pltpu.CompilerParams(vmem_limit_bytes=48 * 1024 * 1024),
        cost_estimate=cost,
    )(*operands, *earlier)


def probs_and_value_grad(first, groups, info, queries, grads, key_window, earlier=None):
    work = groups * GROUP * TOK * WINDOW
    return part_call(
        probs_kernel,
        first,
        groups,
        [info, queries, grads, *key_window],
        [pl.BlockSpec(memory_space=pltpu.SMEM), head_spec(first), head_spec(first)] + window_specs(first),
        [jax.ShapeDtypeStruct((HQ // 2, WINDOW, 2 * TOK), jnp.bfloat16)] + SUMS,
        [probs_spec(first)] + sum_specs(first),
        [
            pltpu.VMEM((WINDOW, TOK), jnp.float32),
            pltpu.VMEM((WINDOW, HD), jnp.float32),
            pltpu.VMEM((WINDOW, HD), jnp.bfloat16),
        ]
        + [pltpu.VMEM((WINDOW, 2 * TOK), jnp.float32)] * 2,
        earlier,
        pl.CostEstimate(flops=4 * work * HD, bytes_accessed=groups * (6 << 20), transcendentals=work),
    )


def query_and_key_grad(first, groups, queries, grads, probs, key_window, value_window, earlier=None):
    work = groups * GROUP * TOK * WINDOW
    return part_call(
        grads_kernel,
        first,
        groups,
        [queries, grads, probs, *key_window, *value_window],
        [head_spec(first), head_spec(first), probs_spec(first)] + window_specs(first) * 2,
        [jax.ShapeDtypeStruct((TOK, HQ * HD), jnp.bfloat16)] + SUMS,
        [head_spec(first)] + sum_specs(first),
        [
            pltpu.VMEM((WINDOW, HD), jnp.float32),
            pltpu.VMEM((WINDOW, HD), jnp.bfloat16),
            pltpu.VMEM((HD, WINDOW), jnp.bfloat16),
        ]
        + [pltpu.VMEM((WINDOW, 2 * TOK), jnp.float32)] * 2
        + [pltpu.VMEM((WINDOW, 2 * TOK), jnp.bfloat16)] * 2,
        earlier,
        pl.CostEstimate(flops=6 * work * HD, bytes_accessed=groups * (7 << 20), transcendentals=0),
    )


def quarter_columns(mine, offset, chip):
    start = (4 * chip + jnp.bitwise_xor(mine, offset)) * SLAB
    return pl.ds(pl.multiple_of(start, SLAB), SLAB)


def quarters_kernel(mine_ref, whole_ref, *quarter_refs):
    for offset, quarter_ref in enumerate(quarter_refs):
        for chip in range(CHIPS):
            quarter_ref[:, chip * SLAB : (chip + 1) * SLAB] = whole_ref[:, quarter_columns(mine_ref[0], offset, chip)]


def interleave_kernel(long_ref, short_ref, out_ref):
    places = short_ref.shape[1] // TOK
    long = long_ref.shape[1] // places
    for place in range(places):
        start = place * (long + TOK)
        out_ref[:, start : start + long] = long_ref[:, place * long : (place + 1) * long]
        out_ref[:, start + long : start + long + TOK] = short_ref[:, place * TOK : (place + 1) * TOK]


def interleaved(long, short):
    return pl.pallas_call(
        interleave_kernel,
        in_specs=[pl.BlockSpec(memory_space=pltpu.VMEM)] * 2,
        out_specs=pl.BlockSpec(memory_space=pltpu.VMEM),
        out_shape=jax.ShapeDtypeStruct((TOK, long.shape[1] + short.shape[1]), jnp.bfloat16),
        cost_estimate=pl.CostEstimate(flops=0, bytes_accessed=4 << 20, transcendentals=0),
    )(long, short)


def quarters_of(mine, whole):
    return pl.pallas_call(
        quarters_kernel,
        in_specs=[pl.BlockSpec(memory_space=pltpu.SMEM), pl.BlockSpec(memory_space=pltpu.VMEM)],
        out_specs=[pl.BlockSpec(memory_space=pltpu.VMEM)] * 4,
        out_shape=[jax.ShapeDtypeStruct((TOK, CHIPS * SLAB), jnp.bfloat16)] * 4,
        cost_estimate=pl.CostEstimate(flops=0, bytes_accessed=4 << 20, transcendentals=0),
    )(mine, whole)


def permuted(value, steps):
    count = lax.axis_size("fsdp")
    return lax.ppermute(value, "fsdp", [(source, (source + steps) % count) for source in range(count)])


def core_swapped(value):
    count = lax.axis_size("fsdp")
    return lax.ppermute(value, "fsdp", [(source, source ^ 1) for source in range(count)])


def quad_partner(value, offset, back=0):
    core, micro = offset // 2, offset % 2
    sections, places = lax.axis_size("pipe"), CHIPS * CORES
    moves = [
        (
            ((section * places) + place) * REPS + rep,
            (((section - back) * places) + (place ^ core)) * REPS + (rep ^ micro),
        )
        for section in range(back, sections)
        for place in range(places)
        for rep in range(REPS)
    ]
    return lax.ppermute(value, ("pipe", "fsdp", "rep"), moves)


def rounded(value):
    return value.astype(jnp.bfloat16)


def after(value, *earlier):
    return lax.optimization_barrier((value, earlier))[0]


def window_of(block, odd, beside=()):
    own = [block]
    for hop in range(HOPS):
        own.append(permuted(own[-1], CORES))
        if hop == 0 and beside:
            own[-1] = after(own[-1], *beside)
    given = jnp.concatenate([lax.select(odd, own[hop + 1], own[hop]) for hop in range(HOPS)], axis=0)
    return own + [core_swapped(given)]


def chip_sums(given, kept, odd):
    taken = core_swapped(given).astype(jnp.float32).reshape(HOPS, TOK, -1)
    kept = kept.reshape(HOPS + 1, TOK, -1)
    none = jnp.zeros((1,) + taken.shape[1:], taken.dtype)
    kept = kept + lax.select(odd, jnp.concatenate([none, taken]), jnp.concatenate([taken, none]))
    return [kept[hop] for hop in range(HOPS)] + [rounded(kept[HOPS])]


def relayed_sum(sums, beside=()):
    total = sums[HOPS]
    for step in range(HOPS):
        arrived = after(permuted(total, -CORES), *beside[step : step + 1])
        total = rounded(sums[HOPS - 1 - step] + arrived.astype(jnp.float32))
    return total


def shards(activations, query_rows, key_rows, out_grad, value_weight, doc_lengths):
    inputs = activations[0, 0]
    queries = query_rows[0, 0]
    keys = key_rows[0, 0]
    grads = out_grad[0, 0]
    weight_rows = value_weight[0]
    place = lax.axis_index("fsdp")
    core, micro = place % CORES, lax.axis_index("rep")
    odd = core == 1
    mine = (REPS * core + micro).reshape(1).astype(jnp.int32)
    info = jnp.concatenate([(place * TOK).reshape(1), doc_lengths[0]]).astype(jnp.int32)
    columns = [list(range(start, CHIPS * CORES, CORES)) for start in range(CORES)]

    weight = lax.all_gather(weight_rows, "fsdp", axis=0, tiled=True)
    quarters = quarters_of(mine, inputs)
    quad_inputs = [quarters[0]] + [quad_partner(quarters[offset], offset) for offset in range(1, 4)]
    key_window = window_of(keys, odd, quarters)

    moves = [(section, section - 1) for section in range(1, lax.axis_size("pipe"))]
    share = lax.ppermute(weight_rows[-TOK:], "pipe", moves)
    info = after(info, share)
    probs, given, kept = probs_and_value_grad(0, KV, info, queries, grads, key_window)
    next_weight = lax.all_gather(after(share, given), "fsdp", axis=0, tiled=True)
    sums = chip_sums(after(given, *quad_inputs[1:]), kept, odd)
    values = rounded(dot(inputs, after(weight, sums[HOPS]), NN))
    value_window = window_of(values, odd)
    value_grad = relayed_sum(sums, [values, *value_window[1:HOPS]])

    sent_weight = weight.reshape(CHIPS * CORES, -1, weight.shape[1])[:, :-TOK].reshape(-1, weight.shape[1])
    input_grad = rounded(dot(value_grad, sent_weight, NT))
    arrived = lax.ppermute(input_grad, "pipe", moves)
    next_grad = lax.ppermute(value_grad, "pipe", moves)
    upstream = interleaved(arrived, rounded(dot(next_grad, next_weight, NT)))

    quad_grads = [value_grad] + [quad_partner(value_grad, offset) for offset in range(1, 4)]
    quad_grads = jnp.concatenate(after(quad_grads, *value_window, input_grad), axis=0)
    weight_part = rounded(dot(jnp.concatenate(quad_inputs, axis=0), quad_grads, TN))
    weight_half = lax.psum_scatter(
        weight_part, "fsdp", scatter_dimension=0, tiled=True, axis_index_groups=columns
    )
    other_half = lax.ppermute(weight_half, "rep", [(0, 1), (1, 0)])
    first = lax.select(micro == 0, weight_half, other_half)
    second = lax.select(micro == 0, other_half, weight_half)
    weight_grad = jnp.concatenate([first, second], axis=0)

    value_window[0] = after(value_window[0], weight_part)
    query_out, given, kept = query_and_key_grad(0, KV, queries, grads, probs, key_window, value_window)
    key_grad = relayed_sum(chip_sums(given, kept, odd), [given, arrived, (upstream, weight_half)])
    return (
        upstream[None, None],
        query_out[None, None],
        key_grad[None, None],
        weight_grad[None],
    )


def solution(mesh):
    tokens = P("pipe", "rep", "fsdp", None)
    weights = P("pipe", "fsdp", None)
    return jax.shard_map(
        shards,
        mesh=mesh,
        in_specs=(tokens, tokens, tokens, tokens, weights, P("rep", None)),
        out_specs=(tokens, tokens, tokens, weights),
        check_vma=False,
    )
```
